512 devices in a mesh: ctx: 64 (over x, z), tp: 8 (over y, core).
Axes of the slice: x: 4, y: 4, z: 16, core: 2. Of those that a mesh axis runs over, the one named last changes fastest.
Arguments:
- queries: bfloat16 [16384, 4096], P('ctx', 'tp'), may hold values from -8 to 8
- key_rows: bfloat16 [16384, 1024], P('ctx', 'tp'), may hold values from -6 to 6
- value_rows: bfloat16 [16384, 1024], P('ctx', 'tp'), may hold values from -6 to 6
- lengths: int32 [64], replicated, may hold values from 128 to 256, as said below
- out_weight: bfloat16 [4096, 4096], P('tp'), may hold values from -0.09375 to 0.09375
Outputs:
- projected: bfloat16 [4096, 16384], P('tp', 'ctx')
The draws below stay inside these ranges and needn't reach their ends.
Inputs may be any that keep to these rules, and one draw needn't show every extreme that they name: `lengths`: multiples of 128, never rising from one shard to the next; the first equals 256 and the last equals 128.
All inputs are finite; a program needn't handle non-finite values.
Results may differ from the reference program's by a relative error of at most 0.019.
Values may be sent and summed in bfloat16 or wider, within the bound.
A program may use at most 128 MiB of HBM per device.

```python
import jax
import jax.numpy as jnp
from jax import lax

D = 4096
HEADS = 32
KV_HEADS = 8
HEAD = 128
CAP = 256
BLOCK = 128
SHARDS = 64
SLOTS = 16384
GROUPS = 8


def draw_queries(key, part):
    key = jax.random.fold_in(key, 5)
    base_key = jax.random.fold_in(key, 0)
    slot_total = SHARDS * CAP
    base = jnp.clip(2.0 * jax.random.normal(base_key, (slot_total, HEADS * HEAD), jnp.float32), -8.0, 8.0)
    return base.astype(jnp.bfloat16)


def draw_key_rows(key, part):
    key = jax.random.fold_in(key, 7)
    slot_total = SHARDS * CAP
    base = jnp.clip(1.5 * jax.random.normal(key, (slot_total, KV_HEADS * HEAD), jnp.float32), -6.0, 6.0)
    return base.astype(jnp.bfloat16)


def draw_lengths(key, part):
    key = jax.random.fold_in(key, 11)
    most_blocks = CAP // BLOCK
    picks = jax.random.randint(key, (SHARDS,), 1, most_blocks + 1)
    ordered = -jnp.sort(-picks)
    ordered = ordered.at[0].set(most_blocks).at[SHARDS - 1].set(1)
    return (ordered * BLOCK).astype(jnp.int32)


def steps_of(stream_key, shape, cuts, least, top_value):
    gain, own = 1.0, jax.random.fold_in(stream_key, 6)
    for axis_at, blocks in cuts:
        heights = jnp.exp(jax.random.uniform(jax.random.fold_in(own, axis_at), (blocks,), jnp.float32, least / len(cuts), top_value / len(cuts)))
        gain = gain * jnp.repeat(heights, shape[axis_at] // blocks).reshape([-1 if axis == axis_at else 1 for axis in range(len(shape))])
    return gain


def bell_draw(rng, shape, deviation, limit, shards=(), held_as=jnp.bfloat16):
    values = deviation * jax.random.normal(rng, shape, jnp.float32)
    if shards:
        values = values * steps_of(rng, shape, shards, -0.22, 0.18)
    return jnp.clip(values, -limit, limit).astype(held_as)


def setup_inputs(seed: int = 0) -> dict:
    splits = jax.random.split(jax.random.key(seed), 6)
    queries = draw_queries(jax.random.fold_in(splits[5], 71), 0)
    key_rows = draw_key_rows(jax.random.fold_in(splits[5], 71), 0)
    value_rows = bell_draw(splits[2], (SLOTS, KV_HEADS * HEAD), 1.0, 6.0, ((0, 64), (1, 8)))
    lengths = draw_lengths(jax.random.fold_in(splits[5], 71), 0)
    out_weight = bell_draw(splits[4], (HEADS * HEAD, D), (HEADS * HEAD) ** -0.5, 0.09375, ((0, 8),))
    return dict(queries=queries, key_rows=key_rows, value_rows=value_rows, lengths=lengths, out_weight=out_weight)


floor_value = -1.0e30


def reference(queries, key_rows, value_rows, lengths, out_weight):
    group_size = HEADS // KV_HEADS
    offsets = jnp.arange(CAP, dtype=jnp.int32)
    starts = (jnp.cumsum(lengths) - lengths).astype(jnp.int32)
    positions = starts[:, None] + offsets[None, :]
    live_slots = offsets[None, :] < lengths[:, None]
    key_heads = key_rows.reshape(SHARDS, CAP, KV_HEADS, HEAD)
    value_heads = value_rows.reshape(SHARDS, CAP, KV_HEADS, HEAD)
    query_heads = queries.reshape(SHARDS, CAP, KV_HEADS, group_size, HEAD)
    scale = HEAD ** -0.5

    def one_shard(shard):
        query_block = lax.dynamic_index_in_dim(query_heads, shard, 0, keepdims=False).astype(jnp.float32)
        query_pos = lax.dynamic_index_in_dim(positions, shard, 0, keepdims=False)

        def scores_for(other):
            keys_here = lax.dynamic_index_in_dim(key_heads, other, 0, keepdims=False).astype(jnp.float32)
            scores = jnp.einsum("qhgd,khd->hgqk", query_block, keys_here) * scale
            key_pos = lax.dynamic_index_in_dim(positions, other, 0, keepdims=False)
            key_live = lax.dynamic_index_in_dim(live_slots, other, 0, keepdims=False)
            allowed = key_live[None, None, None, :] & (key_pos[None, None, None, :] <= query_pos[None, None, :, None])
            return scores, allowed

        def max_step(other, running):
            scores, allowed = scores_for(other)
            return jnp.maximum(running, jnp.max(jnp.where(allowed, scores, floor_value), axis=3))

        start_max = jnp.full((KV_HEADS, group_size, CAP), floor_value, jnp.float32)
        row_max = lax.fori_loop(jnp.int32(0), shard + 1, max_step, start_max)

        def sum_step(other, running):
            total, accum = running
            scores, allowed = scores_for(other)
            expo = jnp.where(allowed, jnp.exp(scores - row_max[..., None]), 0.0)
            weights = lax.optimization_barrier(expo.astype(jnp.bfloat16)).astype(jnp.float32)
            values_here = lax.dynamic_index_in_dim(value_heads, other, 0, keepdims=False).astype(jnp.float32)
            accum = accum + jnp.einsum("hgqk,khd->hgqd", weights, values_here)
            total = total + jnp.sum(expo, axis=3)
            return total, accum

        start_sums = (jnp.zeros((KV_HEADS, group_size, CAP), jnp.float32),
                      jnp.zeros((KV_HEADS, group_size, CAP, HEAD), jnp.float32))
        total, accum = lax.fori_loop(jnp.int32(0), shard + 1, sum_step, start_sums)
        attended = accum / total[..., None]
        live_rows = lax.dynamic_index_in_dim(live_slots, shard, 0, keepdims=False)
        attended = jnp.where(live_rows[None, None, :, None], attended, 0.0)
        return attended.transpose(2, 0, 1, 3).reshape(CAP, HEADS * HEAD).astype(jnp.bfloat16)

    attended = lax.map(one_shard, jnp.arange(SHARDS, dtype=jnp.int32)).reshape(SHARDS * CAP, HEADS * HEAD)
    group_width = HEADS * HEAD // GROUPS
    summed = jnp.zeros((SHARDS * CAP, D), jnp.float32)
    for group_index in range(GROUPS):
        lower_col = group_index * group_width
        partial_sum = jnp.dot(attended[:, lower_col:lower_col + group_width],
                              out_weight[lower_col:lower_col + group_width],
                              preferred_element_type=jnp.float32)
        rounded = lax.optimization_barrier(partial_sum.astype(jnp.bfloat16))
        summed = summed + rounded.astype(jnp.float32)
    return summed.T.astype(jnp.bfloat16)
```

```python
import functools

import jax
import jax.numpy as jnp
from jax import lax
from jax.experimental import pallas as pl
from jax.experimental.pallas import tpu as pltpu
from jax.sharding import PartitionSpec as P

HEAD = 128
BLOCK = 128
NX, NZ, NY = 4, 16, 4
MESH = pl.DeviceIdType.MESH
NEG = -1e30
LOG2E = 1.4426950408889634
F32 = jnp.float32
BF16 = jnp.bfloat16

EDGES = ((0, 2), (0, 1), (2, 4), (2, 3), (4, 5), (5, 6), (6, 7), (7, 8))
ROUNDS = ((1, 2), (3, 4), (5,), (6,), (7,), (8,))


def slot_of(direction, distance):
    if distance == 0:
        return 0
    if distance == 8:
        return 15
    return 2 * distance - 1 if direction == 0 else 2 * distance


def kernel(
    big_rows,
    lengths,
    q_ref,
    k_ref,
    v_ref,
    w_hbm,
    out_ref,
    kvown,
    kvbuf,
    values,
    qown,
    qbuf,
    acc,
    top,
    obuf,
    rbuf,
    merged,
    att,
    wbuf,
    pbuf,
    cbuf,
    sbuf,
    ybuf,
    w_sem,
    kx_send,
    kx_recv,
    qx_send,
    qx_recv,
    ring_send,
    ring_recv,
    o_send,
    o_recv,
    c_send,
    c_recv,
    y_send,
    y_recv,
):
    caps = [256] * big_rows + [128] * (NX - big_rows)
    qts = [cap // NX for cap in caps]
    koff = [4 * sum(qts[:p]) for p in range(NX + 1)]
    qoff = [sum(caps[:p]) for p in range(NX + 1)]
    group_rows = koff[NX]
    heads = q_ref.shape[1] // HEAD
    width = heads * HEAD
    scale = HEAD ** (-0.5) * LOG2E

    ctx = lax.axis_index("ctx")
    tp = lax.axis_index("tp")
    x, z = ctx // NZ, ctx % NZ
    y, core = tp // 2, tp % 2

    def at_x(row):
        return (row * NZ + z, tp)

    def at_z(step):
        return (x * NZ + (z + step + NZ) % NZ, tp)

    def at_y(row):
        return (ctx, row * 2 + core)

    sibling = (ctx, y * 2 + 1 - core)

    classes = []
    if big_rows:
        classes.append((x < big_rows, 256, x * 256))
    if big_rows < NX:
        classes.append((x >= big_rows, 128, big_rows * 256 + (x - big_rows) * 128))

    def by_class(body):
        for condition, cap, first_key in classes:
            run = functools.partial(body, cap, first_key)
            if len(classes) == 1:
                run()
            else:
                pl.when(condition)(run)

    def rows_at(start, size, unit):
        return pl.ds(pl.multiple_of(start, unit), size)

    copy_w = pltpu.make_async_copy(w_hbm, wbuf, w_sem)
    copy_w.start()

    barrier = pltpu.get_barrier_semaphore()
    steps = sorted({b - a for a, b in EDGES})
    partners = [at_x((x + i) % NX) for i in (1, 2, 3)]
    partners += [at_z(sign * step) for step in steps for sign in (1, -1)]
    partners += [at_y((y + i) % NY) for i in (1, 2, 3)]
    partners.append(sibling)
    for partner in partners:
        pl.semaphore_signal(barrier, inc=1, device_id=partner, device_id_type=MESH)

    live_high = lengths[ctx] > BLOCK
    kvown[0:128, 0:HEAD] = k_ref[0:128, :]
    kvown[0:128, HEAD:] = v_ref[0:128, :]
    kvown[128:256, 0:HEAD] = jnp.where(live_high, k_ref[128:256, :], k_ref[0:128, :])
    kvown[128:256, HEAD:] = jnp.where(live_high, v_ref[128:256, :], jnp.zeros((128, HEAD), BF16))

    pl.semaphore_wait(barrier, len(partners))

    def kx_copy(i, cap, first_key):
        qt = cap // NX
        row = (x + i) % NX
        return pltpu.make_async_remote_copy(
            src_ref=kvown.at[rows_at(row * qt, qt, qt)],
            dst_ref=kvbuf.at[rows_at(first_key, qt, qt)],
            send_sem=kx_send.at[i - 1],
            recv_sem=kx_recv.at[x],
            device_id=at_x(row),
            device_id_type=MESH,
        )

    def qx_copy(i, cap):
        return pltpu.make_async_remote_copy(
            src_ref=qown.at[:, 0 : heads * cap],
            dst_ref=qbuf.at[x, :, 0 : heads * cap],
            send_sem=qx_send.at[i - 1],
            recv_sem=qx_recv.at[x],
            device_id=at_x((x + i) % NX),
            device_id_type=MESH,
        )

    @by_class
    def _(cap, first_key):
        qt = cap // NX
        for i in (2, 1, 3):
            kx_copy(i, cap, first_key).start()
        kvbuf[rows_at(first_key, qt, qt), :] = kvown[rows_at(x * qt, qt, qt), :]

    def ring_copy(p, direction, a, b):
        qt = qts[p]

        def rows(distance):
            slot = slot_of(direction, distance)
            start = (slot // 4) * group_rows + koff[p] + (slot % 4) * qt
            return kvbuf.at[start : start + qt]

        return pltpu.make_async_remote_copy(
            src_ref=rows(a),
            dst_ref=rows(b),
            send_sem=ring_send.at[p, direction, b - 1],
            recv_sem=ring_recv.at[p, slot_of(direction, b)],
            device_id=at_z((b - a) if direction == 0 else (a - b)),
            device_id_type=MESH,
        )

    def carried(p, direction, distance):
        return distance < 8 or (p % 2 == direction)

    def forward(p, direction, a):
        for start, end in EDGES:
            if start == a and carried(p, direction, end):
                ring_copy(p, direction, start, end).start()

    for p in range(NX):

        @pl.when(x != p)
        def _(p=p):
            pltpu.make_async_remote_copy(
                src_ref=kvbuf.at[koff[p] : koff[p] + qts[p]],
                dst_ref=kvbuf.at[koff[p] : koff[p] + qts[p]],
                send_sem=kx_send.at[0],
                recv_sem=kx_recv.at[p],
                device_id=at_x((x + 1) % NX),
                device_id_type=MESH,
            ).wait_recv()

        for direction in (0, 1):
            forward(p, direction, 0)

    @by_class
    def _(cap, first_key):
        for h in range(heads):
            turned = q_ref[0:cap, h * HEAD : (h + 1) * HEAD].T
            qown[:, h * cap : (h + 1) * cap] = turned
            qbuf[x, :, h * cap : (h + 1) * cap] = turned
        for i in (2, 1, 3):
            qx_copy(i, cap).start()

    for p in range(NX):
        qt = qts[p]
        for g in range(4):
            lanes = slice(g * group_rows + koff[p], g * group_rows + koff[p] + 4 * qt)
            if caps[p] == BLOCK:
                values[HEAD:, lanes] = jnp.ones((16, 4 * qt), BF16)
                continue
            place = lax.broadcasted_iota(jnp.int32, (16, 4 * qt), 1) // qt
            marks = jnp.zeros((16, 4 * qt), F32)
            for turn in range(4):
                slot = 4 * g + turn
                distance = (slot + 1) // 2
                step = -distance if slot % 2 == 1 else distance
                length = lengths[p * NZ + (z + step + NZ) % NZ]
                marks = jnp.where(place == turn, jnp.where(x * qt < length, 1.0, 0.0), marks)
            values[HEAD:, lanes] = marks.astype(BF16)

    def ring_round(distances):
        for distance in distances:
            for p in range(NX):
                for direction in (0, 1):
                    if not carried(p, direction, distance):
                        continue
                    source = [a for a, b in EDGES if b == distance][0]
                    ring_copy(p, direction, source, distance).wait_recv()
                    forward(p, direction, distance)

    def need_queries(p):
        @pl.when(x != p)
        def _():
            pltpu.make_async_remote_copy(
                src_ref=qbuf.at[p, :, 0 : heads * caps[p]],
                dst_ref=qbuf.at[p, :, 0 : heads * caps[p]],
                send_sem=qx_send.at[0],
                recv_sem=qx_recv.at[p],
                device_id=at_x((x + 1) % NX),
                device_id_type=MESH,
            ).wait_recv()

    def turn_values(g):
        lanes = slice(g * group_rows, (g + 1) * group_rows)
        values[0:HEAD, lanes] = kvbuf[lanes, HEAD:].T

    def attend(g, p):
        cap, qt = caps[p], qts[p]
        before, total = koff[p], koff[p + 1]
        base = g * group_rows
        count = heads * cap
        columns = slice(heads * qoff[p], heads * qoff[p] + count)
        scores = jnp.dot(
            kvbuf[base : base + total, 0:HEAD],
            qbuf[p, :, 0:count],
            preferred_element_type=F32,
        )
        row = lax.broadcasted_iota(jnp.int32, (4 * qt, 1), 0)
        slot = 4 * g + row // qt
        distance = (slot + 1) // 2
        earlier = jnp.where(slot % 2 == 1, z - distance, z + distance - NZ) >= 0
        place = jnp.where(earlier, -1, 100000)
        if g == 0:
            place = jnp.where(slot == 0, x * qt + row % qt, place)
        query = lax.broadcasted_iota(jnp.int32, (4 * qt, count), 1) % cap
        same = jnp.where(place <= query, scores[before:], NEG)
        if before:
            scores = jnp.concatenate([scores[:before], same], axis=0)
        else:
            scores = same
        newest = jnp.max(scores, axis=0, keepdims=True)
        if g:
            old = top[0:1, columns]
            newest = jnp.maximum(old, newest)
        top[0:1, columns] = newest
        weights = jnp.exp2((scores - newest) * scale).astype(BF16)
        fresh = jnp.dot(values[:, base : base + total], weights, preferred_element_type=F32)
        if g:
            fresh = acc[:, columns] * jnp.exp2((old - newest) * scale) + fresh
        acc[:, columns] = fresh

    def o_copy(p, b):
        slot = (x - p + NX) % NX - 1
        return pltpu.make_async_remote_copy(
            src_ref=obuf.at[p, b],
            dst_ref=rbuf.at[slot, b],
            send_sem=o_send.at[p, b],
            recv_sem=o_recv.at[slot, b],
            device_id=at_x(p),
            device_id_type=MESH,
        )

    def finish(p):
        cap = caps[p]
        row = lax.broadcasted_iota(jnp.int32, (16, BLOCK), 0)
        for b in range(cap // BLOCK):
            stats = jnp.zeros((16, BLOCK), F32)
            for h in range(heads):
                start = heads * qoff[p] + h * cap + b * BLOCK
                lanes = slice(start, start + BLOCK)
                total = jnp.maximum(acc[HEAD : HEAD + 1, lanes], 1e-30)
                obuf[p, b, h * HEAD : (h + 1) * HEAD, :] = (
                    acc[0:HEAD, lanes] * (1.0 / total)
                ).astype(BF16)
                level = top[0:1, lanes] * scale + jnp.log2(total)
                high = level.astype(BF16).astype(F32)
                rest = level - high
                middle = rest.astype(BF16).astype(F32)
                low = rest - middle
                stats = jnp.where(row == h, high, stats)
                stats = jnp.where(row == h + 4, middle, stats)
                stats = jnp.where(row == h + 8, low, stats)
            obuf[p, b, width:, :] = stats.astype(BF16)

            @pl.when(x != p)
            def _(b=b):
                o_copy(p, b).start()

    ring_round(ROUNDS[0])
    turn_values(0)
    for p in range(NX):
        need_queries(p)
        attend(0, p)
        if p == 1:
            ring_round(ROUNDS[1])
    ring_round(ROUNDS[2])
    turn_values(1)
    attend(1, 0)
    attend(1, 1)
    ring_round(ROUNDS[3])
    attend(1, 2)
    attend(1, 3)
    turn_values(2)
    ring_round(ROUNDS[4])
    for p in range(NX):
        attend(2, p)
    ring_round(ROUNDS[5])
    turn_values(3)
    for p in range(NX):
        attend(3, p)
        finish(p)

    copy_w.wait()

    def o_wait(slot, b):
        pltpu.make_async_remote_copy(
            src_ref=rbuf.at[slot, b],
            dst_ref=rbuf.at[slot, b],
            send_sem=o_send.at[0, 0],
            recv_sem=o_recv.at[slot, b],
            device_id=at_x((x + 1) % NX),
            device_id_type=MESH,
        ).wait_recv()

    def merge(b):
        parts = [obuf.at[x, b]]
        for slot in range(3):
            o_wait(slot, b)
            parts.append(rbuf.at[slot, b])
        live = jnp.where(b * BLOCK < lengths[ctx], 1.0, 0.0)
        stats = [part[width:, :].astype(F32) for part in parts]
        for h in range(heads):
            rows = slice(h * HEAD, (h + 1) * HEAD)
            levels = [s[h : h + 1] + s[h + 4 : h + 5] + s[h + 8 : h + 9] for s in stats]
            peak = functools.reduce(jnp.maximum, levels)
            shares = [jnp.exp2(level - peak) for level in levels]
            mixed = sum(part[rows, :].astype(F32) * share for part, share in zip(parts, shares))
            merged[rows, :] = (mixed * (live / sum(shares))).astype(BF16)
        att[b] = merged[...].T

    def project(b, which):
        target = (1 - core) if which == 0 else core
        for row in range(NY):
            columns = rows_at((2 * row + target) * width, width, width)
            pbuf[b, which, row] = jnp.dot(
                att[b], wbuf[:, columns], preferred_element_type=F32
            ).astype(BF16)

    def c_copy(b):
        return pltpu.make_async_remote_copy(
            src_ref=pbuf.at[b, 0],
            dst_ref=cbuf.at[b],
            send_sem=c_send.at[b],
            recv_sem=c_recv.at[b],
            device_id=sibling,
            device_id_type=MESH,
        )

    def y_copy(b, i):
        return pltpu.make_async_remote_copy(
            src_ref=sbuf.at[b, i - 1],
            dst_ref=ybuf.at[b, 3 - i],
            send_sem=y_send.at[b, i - 1],
            recv_sem=y_recv.at[b, 3 - i],
            device_id=at_y((y + i) % NY),
            device_id_type=MESH,
        )

    @by_class
    def _(cap, first_key):
        blocks = range(cap // BLOCK)
        for b in blocks:
            merge(b)
            project(b, 0)
            c_copy(b).start()
            project(b, 1)
        for b in blocks:
            c_copy(b).wait_recv()
            for i in (2, 1, 3):
                row = (y + i) % NY
                sbuf[b, i - 1] = (pbuf[b, 1, row].astype(F32) + cbuf[b, row].astype(F32)).astype(BF16)
                y_copy(b, i).start()
        for b in blocks:
            result = pbuf[b, 1, y].astype(F32) + cbuf[b, y].astype(F32)
            for i in (1, 2, 3):
                y_copy(b, i).wait_recv()
            for slot in range(3):
                result = result + ybuf[b, slot].astype(F32)
            out_ref[:, b * BLOCK : (b + 1) * BLOCK] = result.T.astype(BF16)
        if cap == BLOCK:
            out_ref[:, BLOCK:] = jnp.zeros((width, BLOCK), BF16)
        for b in blocks:
            c_copy(b).wait_send()
            for i in (1, 2, 3):
                y_copy(b, i).wait_send()
        for i in (1, 2, 3):
            kx_copy(i, cap, first_key).wait_send()
            qx_copy(i, cap).wait_send()

    for p in range(NX):
        for direction in (0, 1):
            for a, b in EDGES:
                if carried(p, direction, b):
                    ring_copy(p, direction, a, b).wait_send()

        @pl.when(x != p)
        def _(p=p):
            for b in range(caps[p] // BLOCK):
                o_copy(p, b).wait_send()


def call(big_rows, lengths, queries, key_rows, value_rows, out_weight):
    slots, width = queries.shape
    model = out_weight.shape[1]
    heads = width // HEAD
    query_rows = 256 * big_rows + 128 * (NX - big_rows)
    vmem = pl.BlockSpec(memory_space=pltpu.VMEM)
    dma = pltpu.SemaphoreType.DMA
    return pl.pallas_call(
        functools.partial(kernel, big_rows),
        out_shape=jax.ShapeDtypeStruct((width, slots), BF16),
        in_specs=[
            pl.BlockSpec(memory_space=pltpu.SMEM),
            vmem,
            vmem,
            vmem,
            pl.BlockSpec(memory_space=pl.ANY),
        ],
        out_specs=vmem,
        scratch_shapes=[
            pltpu.VMEM((slots, 2 * HEAD), BF16),
            pltpu.VMEM((4 * query_rows, 2 * HEAD), BF16),
            pltpu.VMEM((HEAD + 16, 4 * query_rows), BF16),
            pltpu.VMEM((HEAD, heads * slots), BF16),
            pltpu.VMEM((NX, HEAD, heads * slots), BF16),
            pltpu.VMEM((HEAD + 16, heads * query_rows), F32),
            pltpu.VMEM((8, heads * query_rows), F32),
            pltpu.VMEM((NX, 2, width + 16, BLOCK), BF16),
            pltpu.VMEM((3, 2, width + 16, BLOCK), BF16),
            pltpu.VMEM((width, BLOCK), BF16),
            pltpu.VMEM((2, BLOCK, width), BF16),
            pltpu.VMEM((width, model), BF16),
            pltpu.VMEM((2, 2, NY, BLOCK, width), BF16),
            pltpu.VMEM((2, NY, BLOCK, width), BF16),
            pltpu.VMEM((2, 3, BLOCK, width), BF16),
            pltpu.VMEM((2, 3, BLOCK, width), BF16),
            dma,
            dma((3,)),
            dma((NX,)),
            dma((3,)),
            dma((NX,)),
            dma((NX, 2, 8)),
            dma((NX, 16)),
            dma((NX, 2)),
            dma((3, 2)),
            dma((2,)),
            dma((2,)),
            dma((2, 3)),
            dma((2, 3)),
        ],
        compiler_params=pltpu.CompilerParams(
            collective_id=big_rows, has_side_effects=True, vmem_limit_bytes=56 * 2**20
        ),
        name=f"attend_{big_rows}",
    )(lengths, queries, key_rows, value_rows, out_weight)


def shards(queries, key_rows, value_rows, lengths, out_weight):
    long_shards = jnp.sum((lengths > BLOCK).astype(jnp.int32))
    branches = [functools.partial(call, rows) for rows in range(1, NX + 1)]
    return lax.switch(
        (long_shards + NZ - 1) // NZ - 1, branches, lengths, queries, key_rows, value_rows, out_weight
    )


def solution(mesh):
    placed = (P("ctx", "tp"), P("ctx", "tp"), P("ctx", "tp"), P(), P("tp", None))
    return jax.shard_map(
        shards, mesh=mesh, in_specs=placed, out_specs=P("tp", "ctx"), check_vma=False
    )
```

```python
import functools

import jax
import jax.numpy as jnp
from jax import lax
from jax.experimental import pallas as pl
from jax.experimental.pallas import tpu as pltpu
from jax.sharding import PartitionSpec as P

HEAD = 128
BLOCK = 128
NX, NZ, NY = 4, 16, 4
MESH = pl.DeviceIdType.MESH
NEG = -1e30
LOG2E = 1.4426950408889634
F32 = jnp.float32
BF16 = jnp.bfloat16

EDGES = tuple((step, step + 1) for step in range(8))


def slot_of(direction, distance):
    if distance == 0:
        return 0
    if distance == 8:
        return 15
    return 2 * distance - 1 if direction == 0 else 2 * distance


def kernel(
    big_rows,
    lengths,
    q_hbm,
    k_hbm,
    v_hbm,
    w_hbm,
    out_ref,
    q_ref,
    k_ref,
    v_ref,
    kvown,
    kvbuf,
    values,
    qown,
    qbuf,
    acc,
    top,
    obuf,
    rbuf,
    merged,
    att,
    wbuf,
    wsib,
    asib,
    parts,
    sbuf,
    ybuf,
    in_sem,
    w_sem,
    ws_send,
    ws_recv,
    kx_send,
    kx_recv,
    qx_send,
    qx_recv,
    ring_send,
    ring_recv,
    o_send,
    o_recv,
    c_send,
    c_recv,
    y_send,
    y_recv,
):
    caps = [256] * big_rows + [128] * (NX - big_rows)
    qts = [cap // NX for cap in caps]
    koff = [4 * sum(qts[:p]) for p in range(NX + 1)]
    qoff = [sum(caps[:p]) for p in range(NX + 1)]
    group_rows = koff[NX]
    heads = q_ref.shape[1] // HEAD
    width = heads * HEAD
    scale = HEAD ** (-0.5) * LOG2E

    ctx = lax.axis_index("ctx")
    tp = lax.axis_index("tp")
    x, z = ctx // NZ, ctx % NZ
    y, core = tp // 2, tp % 2

    def at_x(row):
        return (row * NZ + z, tp)

    def at_z(step):
        return (x * NZ + (z + step + NZ) % NZ, tp)

    def at_y(row):
        return (ctx, row * 2 + core)

    sibling = (ctx, y * 2 + 1 - core)

    classes = []
    if big_rows:
        classes.append((x < big_rows, 256, x * 256))
    if big_rows < NX:
        classes.append((x >= big_rows, 128, big_rows * 256 + (x - big_rows) * 128))

    def by_class(body):
        for condition, cap, first_key in classes:
            run = functools.partial(body, cap, first_key)
            if len(classes) == 1:
                run()
            else:
                pl.when(condition)(run)

    def rows_at(start, size, unit):
        return pl.ds(pl.multiple_of(start, unit), size)

    loads = [
        pltpu.make_async_copy(source, target, in_sem.at[i])
        for i, (source, target) in enumerate(((k_hbm, k_ref), (v_hbm, v_ref), (q_hbm, q_ref)))
    ]
    for load in loads:
        load.start()
    copy_w = pltpu.make_async_copy(w_hbm, wbuf, w_sem)
    copy_w.start()

    barrier = pltpu.get_barrier_semaphore()
    steps = sorted({b - a for a, b in EDGES})
    partners = [at_x((x + i) % NX) for i in (1, 2, 3)]
    partners += [at_z(sign * step) for step in steps for sign in (1, -1)]
    partners += [at_y((y + i) % NY) for i in (1, 2, 3)]
    partners.append(sibling)
    for partner in partners:
        pl.semaphore_signal(barrier, inc=1, device_id=partner, device_id_type=MESH)

    loads[0].wait()
    loads[1].wait()

    live_high = lengths[ctx] > BLOCK
    kvown[0:128, 0:HEAD] = k_ref[0:128, :]
    kvown[0:128, HEAD:] = v_ref[0:128, :]
    kvown[128:256, 0:HEAD] = jnp.where(live_high, k_ref[128:256, :], k_ref[0:128, :])
    kvown[128:256, HEAD:] = jnp.where(live_high, v_ref[128:256, :], jnp.zeros((128, HEAD), BF16))

    pl.semaphore_wait(barrier, len(partners))

    def kx_copy(i, cap, first_key):
        qt = cap // NX
        row = (x + i) % NX
        return pltpu.make_async_remote_copy(
            src_ref=kvown.at[rows_at(row * qt, qt, qt)],
            dst_ref=kvbuf.at[rows_at(first_key, qt, qt)],
            send_sem=kx_send.at[i - 1],
            recv_sem=kx_recv.at[x],
            device_id=at_x(row),
            device_id_type=MESH,
        )

    def qx_copy(i, cap):
        return pltpu.make_async_remote_copy(
            src_ref=qown.at[:, 0 : heads * cap],
            dst_ref=qbuf.at[x, :, 0 : heads * cap],
            send_sem=qx_send.at[i - 1],
            recv_sem=qx_recv.at[x],
            device_id=at_x((x + i) % NX),
            device_id_type=MESH,
        )

    @by_class
    def _(cap, first_key):
        qt = cap // NX
        for i in (2, 1, 3):
            kx_copy(i, cap, first_key).start()
        kvbuf[rows_at(first_key, qt, qt), :] = kvown[rows_at(x * qt, qt, qt), :]

    @by_class
    def _(cap, first_key):
        loads[2].wait()
        for h in range(heads):
            turned = q_ref[0:cap, h * HEAD : (h + 1) * HEAD].T
            qown[:, h * cap : (h + 1) * cap] = turned
            qbuf[x, :, h * cap : (h + 1) * cap] = turned
        for i in (2, 1, 3):
            qx_copy(i, cap).start()

    def ring_copy(p, direction, a, b):
        qt = qts[p]

        def rows(distance):
            slot = slot_of(direction, distance)
            start = (slot // 4) * group_rows + koff[p] + (slot % 4) * qt
            return kvbuf.at[start : start + qt]

        return pltpu.make_async_remote_copy(
            src_ref=rows(a),
            dst_ref=rows(b),
            send_sem=ring_send.at[p, direction, b - 1],
            recv_sem=ring_recv.at[p, slot_of(direction, b)],
            device_id=at_z((b - a) if direction == 0 else (a - b)),
            device_id_type=MESH,
        )

    def carried(p, direction, distance):
        return distance < 8 or (p % 2 == direction)

    def forward(p, direction, a):
        for start, end in EDGES:
            if start == a and carried(p, direction, end):
                ring_copy(p, direction, start, end).start()

    for p in range(NX):

        @pl.when(x != p)
        def _(p=p):
            pltpu.make_async_remote_copy(
                src_ref=kvbuf.at[koff[p] : koff[p] + qts[p]],
                dst_ref=kvbuf.at[koff[p] : koff[p] + qts[p]],
                send_sem=kx_send.at[0],
                recv_sem=kx_recv.at[p],
                device_id=at_x((x + 1) % NX),
                device_id_type=MESH,
            ).wait_recv()

        for direction in (0, 1):
            forward(p, direction, 0)

    for p in range(NX):
        qt = qts[p]
        for g in range(4):
            lanes = slice(g * group_rows + koff[p], g * group_rows + koff[p] + 4 * qt)
            if caps[p] == BLOCK:
                values[HEAD:, lanes] = jnp.ones((16, 4 * qt), BF16)
                continue
            place = lax.broadcasted_iota(jnp.int32, (16, 4 * qt), 1) // qt
            marks = jnp.zeros((16, 4 * qt), F32)
            for turn in range(4):
                slot = 4 * g + turn
                distance = (slot + 1) // 2
                step = -distance if slot % 2 == 1 else distance
                length = lengths[p * NZ + (z + step + NZ) % NZ]
                marks = jnp.where(place == turn, jnp.where(x * qt < length, 1.0, 0.0), marks)
            values[HEAD:, lanes] = marks.astype(BF16)

    def ring_round(*distances):
        for distance in distances:
            for p in range(NX):
                for direction in (0, 1):
                    if not carried(p, direction, distance):
                        continue
                    source = [a for a, b in EDGES if b == distance][0]
                    ring_copy(p, direction, source, distance).wait_recv()
                    forward(p, direction, distance)

    def need_queries(p):
        @pl.when(x != p)
        def _():
            pltpu.make_async_remote_copy(
                src_ref=qbuf.at[p, :, 0 : heads * caps[p]],
                dst_ref=qbuf.at[p, :, 0 : heads * caps[p]],
                send_sem=qx_send.at[0],
                recv_sem=qx_recv.at[p],
                device_id=at_x((x + 1) % NX),
                device_id_type=MESH,
            ).wait_recv()

    def turn_values(g):
        lanes = slice(g * group_rows, (g + 1) * group_rows)
        values[0:HEAD, lanes] = kvbuf[lanes, HEAD:].T

    def attend(g, p):
        cap, qt = caps[p], qts[p]
        before, total = koff[p], koff[p + 1]
        base = g * group_rows
        count = heads * cap
        columns = slice(heads * qoff[p], heads * qoff[p] + count)
        scores = jnp.dot(
            kvbuf[base : base + total, 0:HEAD],
            qbuf[p, :, 0:count],
            preferred_element_type=F32,
        )
        row = lax.broadcasted_iota(jnp.int32, (4 * qt, 1), 0)
        slot = 4 * g + row // qt
        distance = (slot + 1) // 2
        earlier = jnp.where(slot % 2 == 1, z - distance, z + distance - NZ) >= 0
        place = jnp.where(earlier, -1, 100000)
        if g == 0:
            place = jnp.where(slot == 0, x * qt + row % qt, place)
        query = lax.broadcasted_iota(jnp.int32, (4 * qt, count), 1) % cap
        same = jnp.where(place <= query, scores[before:], NEG)
        if before:
            scores = jnp.concatenate([scores[:before], same], axis=0)
        else:
            scores = same
        newest = jnp.max(scores, axis=0, keepdims=True)
        if g:
            old = top[0:1, columns]
            newest = jnp.maximum(old, newest)
        top[0:1, columns] = newest
        weights = jnp.exp2((scores - newest) * scale).astype(BF16)
        fresh = jnp.dot(values[:, base : base + total], weights, preferred_element_type=F32)
        if g:
            fresh = acc[:, columns] * jnp.exp2((old - newest) * scale) + fresh
        acc[:, columns] = fresh

    def o_copy(p, b):
        slot = (x - p + NX) % NX - 1
        return pltpu.make_async_remote_copy(
            src_ref=obuf.at[p, b],
            dst_ref=rbuf.at[slot, b],
            send_sem=o_send.at[p, b],
            recv_sem=o_recv.at[slot, b],
            device_id=at_x(p),
            device_id_type=MESH,
        )

    def finish(p, b):
        cap = caps[p]
        row = lax.broadcasted_iota(jnp.int32, (16, BLOCK), 0)
        stats = jnp.zeros((16, BLOCK), F32)
        for h in range(heads):
            start = heads * qoff[p] + h * cap + b * BLOCK
            lanes = slice(start, start + BLOCK)
            total = jnp.maximum(acc[HEAD : HEAD + 1, lanes], 1e-30)
            obuf[p, b, h * HEAD : (h + 1) * HEAD, :] = (
                acc[0:HEAD, lanes] * (1.0 / total)
            ).astype(BF16)
            level = top[0:1, lanes] * scale + jnp.log2(total)
            high = level.astype(BF16).astype(F32)
            rest = level - high
            middle = rest.astype(BF16).astype(F32)
            low = rest - middle
            stats = jnp.where(row == h, high, stats)
            stats = jnp.where(row == h + 4, middle, stats)
            stats = jnp.where(row == h + 8, low, stats)
        obuf[p, b, width:, :] = stats.astype(BF16)

        @pl.when(x != p)
        def _():
            o_copy(p, b).start()

    def ws_copy(row, mine):
        target = core if mine else 1 - core
        columns = rows_at((2 * row + target) * width, width, width)
        return pltpu.make_async_remote_copy(
            src_ref=wbuf.at[:, columns],
            dst_ref=wsib.at[row],
            send_sem=ws_send.at[row],
            recv_sem=ws_recv.at[row],
            device_id=sibling,
            device_id_type=MESH,
        )

    ring_round(1, 2)
    turn_values(0)
    copy_w.wait()
    for row in range(NY):
        ws_copy(row, False).start()
    for g in range(4):
        for p in range(NX):
            if g == 0:
                need_queries(p)
            attend(g, p)
            if g == 3:
                finish(p, 0)
            elif p % 2 == 1:
                ring_round(2 * g + 2 + (p + 1) // 2)
                if p == 3:
                    turn_values(g + 1)
    for p in range(big_rows):
        finish(p, 1)
    for row in range(NY):
        ws_copy(row, True).wait_recv()

    def o_wait(slot, b):
        pltpu.make_async_remote_copy(
            src_ref=rbuf.at[slot, b],
            dst_ref=rbuf.at[slot, b],
            send_sem=o_send.at[0, 0],
            recv_sem=o_recv.at[slot, b],
            device_id=at_x((x + 1) % NX),
            device_id_type=MESH,
        ).wait_recv()

    def merge(b):
        parts = [obuf.at[x, b]]
        for slot in range(3):
            o_wait(slot, b)
            parts.append(rbuf.at[slot, b])
        live = jnp.where(b * BLOCK < lengths[ctx], 1.0, 0.0)
        stats = [part[width:, :].astype(F32) for part in parts]
        for h in range(heads):
            rows = slice(h * HEAD, (h + 1) * HEAD)
            levels = [s[h : h + 1] + s[h + 4 : h + 5] + s[h + 8 : h + 9] for s in stats]
            peak = functools.reduce(jnp.maximum, levels)
            shares = [jnp.exp2(level - peak) for level in levels]
            mixed = sum(part[rows, :].astype(F32) * share for part, share in zip(parts, shares))
            merged[rows, :] = (mixed * (live / sum(shares))).astype(BF16)
        att[b] = merged[...].T

    def a_copy(b):
        return pltpu.make_async_remote_copy(
            src_ref=att.at[b],
            dst_ref=asib.at[b],
            send_sem=c_send.at[b],
            recv_sem=c_recv.at[b],
            device_id=sibling,
            device_id_type=MESH,
        )

    def y_copy(b, i):
        return pltpu.make_async_remote_copy(
            src_ref=sbuf.at[b, i - 1],
            dst_ref=ybuf.at[b, 3 - i],
            send_sem=y_send.at[b, i - 1],
            recv_sem=y_recv.at[b, 3 - i],
            device_id=at_y((y + i) % NY),
            device_id_type=MESH,
        )

    def project(b):
        a_copy(b).start()
        for i in (2, 1, 3, 0):
            columns = rows_at((2 * ((y + i) % NY) + core) * width, width, width)
            parts[b, i] = jnp.dot(att[b], wbuf[:, columns], preferred_element_type=F32)
        a_copy(b).wait_recv()
        for i in (2, 1, 3, 0):
            added = jnp.dot(asib[b], wsib[(y + i) % NY], preferred_element_type=F32)
            if i:
                sbuf[b, i - 1] = (parts[b, i] + added).astype(BF16)
                y_copy(b, i).start()
            else:
                parts[b, 0] = parts[b, 0] + added

    @by_class
    def _(cap, first_key):
        blocks = range(cap // BLOCK)
        for b in blocks:
            merge(b)
            project(b)
        for b in blocks:
            result = parts[b, 0]
            for i in (1, 2, 3):
                y_copy(b, i).wait_recv()
            for slot in range(3):
                result = result + ybuf[b, slot].astype(F32)
            out_ref[:, b * BLOCK : (b + 1) * BLOCK] = result.T.astype(BF16)
        if cap == BLOCK:
            out_ref[:, BLOCK:] = jnp.zeros((width, BLOCK), BF16)
        for b in blocks:
            a_copy(b).wait_send()
            for i in (1, 2, 3):
                y_copy(b, i).wait_send()
        for i in (1, 2, 3):
            kx_copy(i, cap, first_key).wait_send()
            qx_copy(i, cap).wait_send()

    for row in range(NY):
        ws_copy(row, False).wait_send()
    for p in range(NX):
        for direction in (0, 1):
            for a, b in EDGES:
                if carried(p, direction, b):
                    ring_copy(p, direction, a, b).wait_send()

        @pl.when(x != p)
        def _(p=p):
            for b in range(caps[p] // BLOCK):
                o_copy(p, b).wait_send()


def call(big_rows, lengths, queries, key_rows, value_rows, out_weight):
    slots, width = queries.shape
    model = out_weight.shape[1]
    heads = width // HEAD
    query_rows = 256 * big_rows + 128 * (NX - big_rows)
    vmem = pl.BlockSpec(memory_space=pltpu.VMEM)
    dma = pltpu.SemaphoreType.DMA
    return pl.pallas_call(
        functools.partial(kernel, big_rows),
        out_shape=jax.ShapeDtypeStruct((width, slots), BF16),
        in_specs=[
            pl.BlockSpec(memory_space=pltpu.SMEM),
            *([pl.BlockSpec(memory_space=pl.ANY)] * 4),
        ],
        out_specs=vmem,
        scratch_shapes=[
            pltpu.VMEM((slots, width), BF16),
            pltpu.VMEM((slots, HEAD), BF16),
            pltpu.VMEM((slots, HEAD), BF16),
            pltpu.VMEM((slots, 2 * HEAD), BF16),
            pltpu.VMEM((4 * query_rows, 2 * HEAD), BF16),
            pltpu.VMEM((HEAD + 16, 4 * query_rows), BF16),
            pltpu.VMEM((HEAD, heads * slots), BF16),
            pltpu.VMEM((NX, HEAD, heads * slots), BF16),
            pltpu.VMEM((HEAD + 16, heads * query_rows), F32),
            pltpu.VMEM((8, heads * query_rows), F32),
            pltpu.VMEM((NX, 2, width + 16, BLOCK), BF16),
            pltpu.VMEM((3, 2, width + 16, BLOCK), BF16),
            pltpu.VMEM((width, BLOCK), BF16),
            pltpu.VMEM((2, BLOCK, width), BF16),
            pltpu.VMEM((width, model), BF16),
            pltpu.VMEM((NY, width, width), BF16),
            pltpu.VMEM((2, BLOCK, width), BF16),
            pltpu.VMEM((2, NY, BLOCK, width), F32),
            pltpu.VMEM((2, 3, BLOCK, width), BF16),
            pltpu.VMEM((2, 3, BLOCK, width), BF16),
            dma((3,)),
            dma,
            dma((NY,)),
            dma((NY,)),
            dma((3,)),
            dma((NX,)),
            dma((3,)),
            dma((NX,)),
            dma((NX, 2, 8)),
            dma((NX, 16)),
            dma((NX, 2)),
            dma((3, 2)),
            dma((2,)),
            dma((2,)),
            dma((2, 3)),
            dma((2, 3)),
        ],
        compiler_params=pltpu.CompilerParams(
            collective_id=big_rows, has_side_effects=True, vmem_limit_bytes=56 * 2**20
        ),
        name=f"attend_{big_rows}",
    )(lengths, queries, key_rows, value_rows, out_weight)


def shards(queries, key_rows, value_rows, lengths, out_weight):
    def at_most(rows, low, high):
        return lambda *held: lax.cond(held[0][rows * NZ] <= BLOCK, low, high, *held)

    low, middle, high = [functools.partial(call, rows) for rows in (2, 3, 4)]
    return at_most(2, low, at_most(3, middle, high))(
        lengths, queries, key_rows, value_rows, out_weight
    )


def solution(mesh):
    placed = (P("ctx", "tp"), P("ctx", "tp"), P("ctx", "tp"), P(), P("tp", None))
    return jax.shard_map(
        shards, mesh=mesh, in_specs=placed, out_specs=P("tp", "ctx"), check_vma=False
    )
```

```python
import functools

import jax
import jax.numpy as jnp
from jax import lax
from jax.experimental import pallas as pl
from jax.experimental.pallas import tpu as pltpu
from jax.sharding import PartitionSpec as P

HEAD = 128
BLOCK = 128
NX, NZ, NY = 4, 16, 4
MESH = pl.DeviceIdType.MESH
NEG = -1e30
LOG2E = 1.4426950408889634
F32 = jnp.float32
BF16 = jnp.bfloat16

EDGES = tuple((step, step + 1) for step in range(8))


def slot_of(direction, distance):
    if distance == 0:
        return 0
    if distance == 8:
        return 15
    return 2 * distance - 1 if direction == 0 else 2 * distance


def kernel(
    big_rows,
    lengths,
    q_hbm,
    k_hbm,
    v_hbm,
    w_hbm,
    out_ref,
    q_ref,
    k_ref,
    v_ref,
    kvown,
    kvbuf,
    values,
    qown,
    qbuf,
    acc,
    top,
    obuf,
    rbuf,
    merged,
    att,
    wbuf,
    wsib,
    asib,
    parts,
    sbuf,
    ybuf,
    in_sem,
    w_sem,
    ws_send,
    ws_recv,
    kx_send,
    kx_recv,
    qx_send,
    qx_recv,
    ring_send,
    ring_recv,
    o_send,
    o_recv,
    c_send,
    c_recv,
    y_send,
    y_recv,
):
    caps = [256] * big_rows + [128] * (NX - big_rows)
    qts = [cap // NX for cap in caps]
    koff = [4 * sum(qts[:p]) for p in range(NX + 1)]
    qoff = [sum(caps[:p]) for p in range(NX + 1)]
    group_rows = koff[NX]
    heads = q_ref.shape[1] // HEAD
    width = heads * HEAD
    scale = HEAD ** (-0.5) * LOG2E

    ctx = lax.axis_index("ctx")
    tp = lax.axis_index("tp")
    x, z = ctx // NZ, ctx % NZ
    y, core = tp // 2, tp % 2

    def at_x(row):
        return (row * NZ + z, tp)

    def at_z(step):
        return (x * NZ + (z + step + NZ) % NZ, tp)

    def at_y(row):
        return (ctx, row * 2 + core)

    sibling = (ctx, y * 2 + 1 - core)

    classes = []
    if big_rows:
        classes.append((x < big_rows, 256, x * 256))
    if big_rows < NX:
        classes.append((x >= big_rows, 128, big_rows * 256 + (x - big_rows) * 128))

    def by_class(body):
        for condition, cap, first_key in classes:
            run = functools.partial(body, cap, first_key)
            if len(classes) == 1:
                run()
            else:
                pl.when(condition)(run)

    def rows_at(start, size, unit):
        return pl.ds(pl.multiple_of(start, unit), size)

    loads = [
        pltpu.make_async_copy(source, target, in_sem.at[i])
        for i, (source, target) in enumerate(((k_hbm, k_ref), (v_hbm, v_ref), (q_hbm, q_ref)))
    ]
    for load in loads:
        load.start()
    copy_w = pltpu.make_async_copy(w_hbm, wbuf, w_sem)
    copy_w.start()

    barrier = pltpu.get_barrier_semaphore()
    steps = sorted({b - a for a, b in EDGES})
    partners = [at_x((x + i) % NX) for i in (1, 2, 3)]
    partners += [at_z(sign * step) for step in steps for sign in (1, -1)]
    partners += [at_y((y + i) % NY) for i in (1, 2, 3)]
    partners.append(sibling)
    for partner in partners:
        pl.semaphore_signal(barrier, inc=1, device_id=partner, device_id_type=MESH)

    loads[0].wait()
    loads[1].wait()

    live_high = lengths[ctx] > BLOCK
    kvown[0:128, 0:HEAD] = k_ref[0:128, :]
    kvown[0:128, HEAD:] = v_ref[0:128, :]
    kvown[128:256, 0:HEAD] = jnp.where(live_high, k_ref[128:256, :], k_ref[0:128, :])
    kvown[128:256, HEAD:] = jnp.where(live_high, v_ref[128:256, :], jnp.zeros((128, HEAD), BF16))

    pl.semaphore_wait(barrier, len(partners))

    def kx_copy(i, cap, first_key):
        qt = cap // NX
        row = (x + i) % NX
        return pltpu.make_async_remote_copy(
            src_ref=kvown.at[rows_at(row * qt, qt, qt)],
            dst_ref=kvbuf.at[rows_at(first_key, qt, qt)],
            send_sem=kx_send.at[i - 1],
            recv_sem=kx_recv.at[x],
            device_id=at_x(row),
            device_id_type=MESH,
        )

    def qx_copy(i, cap):
        return pltpu.make_async_remote_copy(
            src_ref=qown.at[:, 0 : heads * cap],
            dst_ref=qbuf.at[x, :, 0 : heads * cap],
            send_sem=qx_send.at[i - 1],
            recv_sem=qx_recv.at[x],
            device_id=at_x((x + i) % NX),
            device_id_type=MESH,
        )

    @by_class
    def _(cap, first_key):
        qt = cap // NX
        for i in (2, 1, 3):
            kx_copy(i, cap, first_key).start()
        kvbuf[rows_at(first_key, qt, qt), :] = kvown[rows_at(x * qt, qt, qt), :]

    @by_class
    def _(cap, first_key):
        loads[2].wait()
        for h in range(heads):
            turned = q_ref[0:cap, h * HEAD : (h + 1) * HEAD].T
            qown[:, h * cap : (h + 1) * cap] = turned
            qbuf[x, :, h * cap : (h + 1) * cap] = turned
        for i in (2, 1, 3):
            qx_copy(i, cap).start()

    def ring_copy(p, direction, a, b):
        qt = qts[p]

        def rows(distance):
            slot = slot_of(direction, distance)
            start = (slot // 4) * group_rows + koff[p] + (slot % 4) * qt
            return kvbuf.at[start : start + qt]

        return pltpu.make_async_remote_copy(
            src_ref=rows(a),
            dst_ref=rows(b),
            send_sem=ring_send.at[p, direction, b - 1],
            recv_sem=ring_recv.at[p, slot_of(direction, b)],
            device_id=at_z((b - a) if direction == 0 else (a - b)),
            device_id_type=MESH,
        )

    def carried(p, direction, distance):
        return distance < 8 or (p % 2 == direction)

    def forward(p, direction, a):
        for start, end in EDGES:
            if start == a and carried(p, direction, end):
                ring_copy(p, direction, start, end).start()

    for p in range(NX):

        @pl.when(x == p)
        def _(p=p):
            for direction in (0, 1):
                forward(p, direction, 0)

    for p in range(NX):

        @pl.when(x != p)
        def _(p=p):
            pltpu.make_async_remote_copy(
                src_ref=kvbuf.at[koff[p] : koff[p] + qts[p]],
                dst_ref=kvbuf.at[koff[p] : koff[p] + qts[p]],
                send_sem=kx_send.at[0],
                recv_sem=kx_recv.at[p],
                device_id=at_x((x + 1) % NX),
                device_id_type=MESH,
            ).wait_recv()
            for direction in (0, 1):
                forward(p, direction, 0)

    for p in range(NX):
        qt = qts[p]
        for g in range(4):
            lanes = slice(g * group_rows + koff[p], g * group_rows + koff[p] + 4 * qt)
            if caps[p] == BLOCK:
                values[HEAD:, lanes] = jnp.ones((16, 4 * qt), BF16)
                continue
            place = lax.broadcasted_iota(jnp.int32, (16, 4 * qt), 1) // qt
            marks = jnp.zeros((16, 4 * qt), F32)
            for turn in range(4):
                slot = 4 * g + turn
                distance = (slot + 1) // 2
                step = -distance if slot % 2 == 1 else distance
                length = lengths[p * NZ + (z + step + NZ) % NZ]
                marks = jnp.where(place == turn, jnp.where(x * qt < length, 1.0, 0.0), marks)
            values[HEAD:, lanes] = marks.astype(BF16)

    def ring_round(*distances):
        for distance in distances:
            for p in range(NX):
                for direction in (0, 1):
                    if not carried(p, direction, distance):
                        continue
                    source = [a for a, b in EDGES if b == distance][0]
                    ring_copy(p, direction, source, distance).wait_recv()
                    forward(p, direction, distance)

    def need_queries(p):
        @pl.when(x != p)
        def _():
            pltpu.make_async_remote_copy(
                src_ref=qbuf.at[p, :, 0 : heads * caps[p]],
                dst_ref=qbuf.at[p, :, 0 : heads * caps[p]],
                send_sem=qx_send.at[0],
                recv_sem=qx_recv.at[p],
                device_id=at_x((x + 1) % NX),
                device_id_type=MESH,
            ).wait_recv()

    def turn_values(g):
        lanes = slice(g * group_rows, (g + 1) * group_rows)
        values[0:HEAD, lanes] = kvbuf[lanes, HEAD:].T

    def attend(g, p):
        cap, qt = caps[p], qts[p]
        before, total = koff[p], koff[p + 1]
        base = g * group_rows
        count = heads * cap
        columns = slice(heads * qoff[p], heads * qoff[p] + count)
        scores = jnp.dot(
            kvbuf[base : base + total, 0:HEAD],
            qbuf[p, :, 0:count],
            preferred_element_type=F32,
        )
        row = lax.broadcasted_iota(jnp.int32, (4 * qt, 1), 0)
        slot = 4 * g + row // qt
        distance = (slot + 1) // 2
        earlier = jnp.where(slot % 2 == 1, z - distance, z + distance - NZ) >= 0
        place = jnp.where(earlier, -1, 100000)
        if g == 0:
            place = jnp.where(slot == 0, x * qt + row % qt, place)
        query = lax.broadcasted_iota(jnp.int32, (4 * qt, count), 1) % cap
        same = jnp.where(place <= query, scores[before:], NEG)
        if before:
            scores = jnp.concatenate([scores[:before], same], axis=0)
        else:
            scores = same
        newest = jnp.max(scores, axis=0, keepdims=True)
        if g:
            old = top[0:1, columns]
            newest = jnp.maximum(old, newest)
        top[0:1, columns] = newest
        weights = jnp.exp2((scores - newest) * scale).astype(BF16)
        fresh = jnp.dot(values[:, base : base + total], weights, preferred_element_type=F32)
        if g:
            fresh = acc[:, columns] * jnp.exp2((old - newest) * scale) + fresh
        acc[:, columns] = fresh

    def o_copy(p, b):
        slot = (x - p + NX) % NX - 1
        return pltpu.make_async_remote_copy(
            src_ref=obuf.at[p, b],
            dst_ref=rbuf.at[slot, b],
            send_sem=o_send.at[p, b],
            recv_sem=o_recv.at[slot, b],
            device_id=at_x(p),
            device_id_type=MESH,
        )

    def finish(p, b):
        cap = caps[p]
        row = lax.broadcasted_iota(jnp.int32, (16, BLOCK), 0)
        stats = jnp.zeros((16, BLOCK), F32)
        for h in range(heads):
            start = heads * qoff[p] + h * cap + b * BLOCK
            lanes = slice(start, start + BLOCK)
            total = jnp.maximum(acc[HEAD : HEAD + 1, lanes], 1e-30)
            obuf[p, b, h * HEAD : (h + 1) * HEAD, :] = (
                acc[0:HEAD, lanes] * (1.0 / total)
            ).astype(BF16)
            level = top[0:1, lanes] * scale + jnp.log2(total)
            high = level.astype(BF16).astype(F32)
            rest = level - high
            middle = rest.astype(BF16).astype(F32)
            low = rest - middle
            stats = jnp.where(row == h, high, stats)
            stats = jnp.where(row == h + 4, middle, stats)
            stats = jnp.where(row == h + 8, low, stats)
        obuf[p, b, width:, :] = stats.astype(BF16)

        @pl.when(x != p)
        def _():
            o_copy(p, b).start()

    def ws_copy(row, mine):
        target = core if mine else 1 - core
        columns = rows_at((2 * row + target) * width, width, width)
        return pltpu.make_async_remote_copy(
            src_ref=wbuf.at[:, columns],
            dst_ref=wsib.at[row],
            send_sem=ws_send.at[row],
            recv_sem=ws_recv.at[row],
            device_id=sibling,
            device_id_type=MESH,
        )

    ring_round(1, 2)
    turn_values(0)
    copy_w.wait()
    for row in range(NY):
        ws_copy(row, False).start()
    for g in range(4):
        for p in range(NX):
            if g == 0:
                need_queries(p)
            attend(g, p)
            if g == 3:
                finish(p, 0)
                if p == big_rows - 1:
                    for row in range(big_rows):
                        finish(row, 1)
            elif p % 2 == 1:
                ring_round(2 * g + 2 + (p + 1) // 2)
                if p == 3:
                    turn_values(g + 1)
    for row in range(NY):
        ws_copy(row, True).wait_recv()

    def o_wait(slot, b):
        pltpu.make_async_remote_copy(
            src_ref=rbuf.at[slot, b],
            dst_ref=rbuf.at[slot, b],
            send_sem=o_send.at[0, 0],
            recv_sem=o_recv.at[slot, b],
            device_id=at_x((x + 1) % NX),
            device_id_type=MESH,
        ).wait_recv()

    def merge(b):
        parts = [obuf.at[x, b]]
        for slot in range(3):
            o_wait(slot, b)
            parts.append(rbuf.at[slot, b])
        live = jnp.where(b * BLOCK < lengths[ctx], 1.0, 0.0)
        stats = [part[width:, :].astype(F32) for part in parts]
        for h in range(heads):
            rows = slice(h * HEAD, (h + 1) * HEAD)
            levels = [s[h : h + 1] + s[h + 4 : h + 5] + s[h + 8 : h + 9] for s in stats]
            peak = functools.reduce(jnp.maximum, levels)
            shares = [jnp.exp2(level - peak) for level in levels]
            mixed = sum(part[rows, :].astype(F32) * share for part, share in zip(parts, shares))
            merged[rows, :] = (mixed * (live / sum(shares))).astype(BF16)
        att[b] = merged[...].T

    def a_copy(b):
        return pltpu.make_async_remote_copy(
            src_ref=att.at[b],
            dst_ref=asib.at[b],
            send_sem=c_send.at[b],
            recv_sem=c_recv.at[b],
            device_id=sibling,
            device_id_type=MESH,
        )

    def y_copy(b, i):
        return pltpu.make_async_remote_copy(
            src_ref=sbuf.at[b, i - 1],
            dst_ref=ybuf.at[b, 3 - i],
            send_sem=y_send.at[b, i - 1],
            recv_sem=y_recv.at[b, 3 - i],
            device_id=at_y((y + i) % NY),
            device_id_type=MESH,
        )

    def project(b):
        a_copy(b).start()
        for i in (2, 1, 3, 0):
            columns = rows_at((2 * ((y + i) % NY) + core) * width, width, width)
            parts[b, i] = jnp.dot(att[b], wbuf[:, columns], preferred_element_type=F32)
        a_copy(b).wait_recv()
        for i in (2, 1, 3, 0):
            added = jnp.dot(asib[b], wsib[(y + i) % NY], preferred_element_type=F32)
            if i:
                sbuf[b, i - 1] = (parts[b, i] + added).astype(BF16)
                y_copy(b, i).start()
            else:
                parts[b, 0] = parts[b, 0] + added

    @by_class
    def _(cap, first_key):
        blocks = range(cap // BLOCK)
        for b in blocks:
            merge(b)
            project(b)
        for b in blocks:
            result = parts[b, 0]
            for i in (1, 2, 3):
                y_copy(b, i).wait_recv()
            for slot in range(3):
                result = result + ybuf[b, slot].astype(F32)
            out_ref[:, b * BLOCK : (b + 1) * BLOCK] = result.T.astype(BF16)
        if cap == BLOCK:
            out_ref[:, BLOCK:] = jnp.zeros((width, BLOCK), BF16)
        for b in blocks:
            a_copy(b).wait_send()
            for i in (1, 2, 3):
                y_copy(b, i).wait_send()
        for i in (1, 2, 3):
            kx_copy(i, cap, first_key).wait_send()
            qx_copy(i, cap).wait_send()

    for row in range(NY):
        ws_copy(row, False).wait_send()
    for p in range(NX):
        for direction in (0, 1):
            for a, b in EDGES:
                if carried(p, direction, b):
                    ring_copy(p, direction, a, b).wait_send()

        @pl.when(x != p)
        def _(p=p):
            for b in range(caps[p] // BLOCK):
                o_copy(p, b).wait_send()


def call(big_rows, lengths, queries, key_rows, value_rows, out_weight):
    slots, width = queries.shape
    model = out_weight.shape[1]
    heads = width // HEAD
    query_rows = 256 * big_rows + 128 * (NX - big_rows)
    vmem = pl.BlockSpec(memory_space=pltpu.VMEM)
    dma = pltpu.SemaphoreType.DMA
    return pl.pallas_call(
        functools.partial(kernel, big_rows),
        out_shape=jax.ShapeDtypeStruct((width, slots), BF16),
        in_specs=[
            pl.BlockSpec(memory_space=pltpu.SMEM),
            *([pl.BlockSpec(memory_space=pl.ANY)] * 4),
        ],
        out_specs=vmem,
        scratch_shapes=[
            pltpu.VMEM((slots, width), BF16),
            pltpu.VMEM((slots, HEAD), BF16),
            pltpu.VMEM((slots, HEAD), BF16),
            pltpu.VMEM((slots, 2 * HEAD), BF16),
            pltpu.VMEM((4 * query_rows, 2 * HEAD), BF16),
            pltpu.VMEM((HEAD + 16, 4 * query_rows), BF16),
            pltpu.VMEM((HEAD, heads * slots), BF16),
            pltpu.VMEM((NX, HEAD, heads * slots), BF16),
            pltpu.VMEM((HEAD + 16, heads * query_rows), F32),
            pltpu.VMEM((8, heads * query_rows), F32),
            pltpu.VMEM((NX, 2, width + 16, BLOCK), BF16),
            pltpu.VMEM((3, 2, width + 16, BLOCK), BF16),
            pltpu.VMEM((width, BLOCK), BF16),
            pltpu.VMEM((2, BLOCK, width), BF16),
            pltpu.VMEM((width, model), BF16),
            pltpu.VMEM((NY, width, width), BF16),
            pltpu.VMEM((2, BLOCK, width), BF16),
            pltpu.VMEM((2, NY, BLOCK, width), F32),
            pltpu.VMEM((2, 3, BLOCK, width), BF16),
            pltpu.VMEM((2, 3, BLOCK, width), BF16),
            dma((3,)),
            dma,
            dma((NY,)),
            dma((NY,)),
            dma((3,)),
            dma((NX,)),
            dma((3,)),
            dma((NX,)),
            dma((NX, 2, 8)),
            dma((NX, 16)),
            dma((NX, 2)),
            dma((3, 2)),
            dma((2,)),
            dma((2,)),
            dma((2, 3)),
            dma((2, 3)),
        ],
        compiler_params=pltpu.CompilerParams(
            collective_id=big_rows, has_side_effects=True, vmem_limit_bytes=56 * 2**20
        ),
        name=f"attend_{big_rows}",
    )(lengths, queries, key_rows, value_rows, out_weight)


def shards(queries, key_rows, value_rows, lengths, out_weight):
    def at_most(rows, low, high):
        return lambda *held: lax.cond(held[0][rows * NZ] <= BLOCK, low, high, *held)

    low, middle, high = [functools.partial(call, rows) for rows in (2, 3, 4)]
    return at_most(2, low, at_most(3, middle, high))(
        lengths, queries, key_rows, value_rows, out_weight
    )


def solution(mesh):
    placed = (P("ctx", "tp"), P("ctx", "tp"), P("ctx", "tp"), P(), P("tp", None))
    return jax.shard_map(
        shards, mesh=mesh, in_specs=placed, out_specs=P("tp", "ctx"), check_vma=False
    )
```
